256 devices in a mesh: dp: 16 (over z_lo, y), et: 16 (over z_hi, x, core).
Axes of the slice: x: 4, y: 4, z: 8 (z_hi: 2, z_lo: 4; z = z_hi * 4 + z_lo), core: 2. Of those that a mesh axis runs over, the one named last changes fastest.
Arguments:
- tokens: bfloat16 [2048, 4096], P('dp'), may hold values from -6 to 6
- expert_ids: int32 [2048, 2], P('dp'), may hold values from 0 to 7, as said below
- gate_fixed: int32 [2048, 2], P('dp'), may hold values from 1 to 32767
- w_gate: bfloat16 [2, 4096, 14336], P(None, 'dp', 'et'), may hold values from -0.09375 to 0.09375
- w_up: bfloat16 [2, 4096, 14336], P(None, 'dp', 'et'), may hold values from -0.09375 to 0.09375
- w_down: bfloat16 [2, 14336, 4096], P(None, 'et', 'dp'), may hold values from -0.046875 to 0.046875
- d_out: bfloat16 [2048, 4096], P('dp'), may hold values from -6 to 6
Outputs:
- mixed: float32 [2048, 4096], P('dp', 'et')
- grad_tokens: float32 [2048, 4096], P('dp', 'et')
- grad_gate: float32 [2, 4096, 14336], P(None, 'dp', 'et')
- grad_up: float32 [2, 4096, 14336], P(None, 'dp', 'et')
- grad_down: float32 [2, 14336, 4096], P(None, 'et', 'dp')
The draws below stay inside these ranges and needn't reach their ends.
Inputs may be any that keep to these rules, and one draw needn't show every extreme that they name: `expert_ids`: each row names two different experts. Among the 128 tokens of one index of dp, at most 32 name any one expert below 2, and for each such expert some index reaches 32 in every draw.
All inputs are finite; a program needn't handle non-finite values.
Results may differ from the reference program's by a relative error of at most 0.0041.
Values may be sent and summed in bfloat16 or wider, within the bound.
No kernel may reach another device: no remote copies, remote signals or barrier semaphores. Data moves between devices by JAX's collectives and lax.ppermute only.
A program may use at most 64 MiB of HBM per device.

```python
import jax
import jax.numpy as jnp
from jax import lax

D = 4096
FF = 14336
EXPERTS_ALL = 8
EXPERTS = 2
CAP = 32
TOK_DEV = 128
TOKENS = 2048
N_DP = 16


def draw_expert_ids(key, part):
    groups = TOKENS // TOK_DEV
    others = EXPERTS_ALL - EXPERTS
    keys = jax.random.split(key, 6)
    counts = jax.random.randint(keys[0], (groups, 2), CAP // 4, CAP + 1)
    fullest = jax.random.randint(keys[1], (2,), 0, groups)
    group_range = jnp.arange(groups, dtype=jnp.int32)
    counts = jnp.where(group_range[:, None] == fullest[None, :], CAP, counts)
    scores = jax.random.randint(keys[2], (groups, 2, TOK_DEV), 0, 1 << 20) * TOK_DEV + jnp.arange(TOK_DEV, dtype=jnp.int32)
    order = jnp.argsort(scores, axis=2)
    ranks = jnp.argsort(order, axis=2)
    chosen = ranks < counts[:, :, None]
    first_other = jax.random.randint(keys[3], (groups, TOK_DEV), 0, others)
    second_other = (first_other + jax.random.randint(keys[4], (groups, TOK_DEV), 1, others)) % others
    pick_zero = jnp.where(chosen[:, 0, :], 0, EXPERTS + first_other)
    pick_one = jnp.where(chosen[:, 1, :], 1, EXPERTS + second_other)
    flipped = jax.random.randint(keys[5], (groups, TOK_DEV), 0, 2) == 1
    first_pick = jnp.where(flipped, pick_one, pick_zero)
    second_pick = jnp.where(flipped, pick_zero, pick_one)
    return jnp.stack([first_pick, second_pick], axis=2).reshape(TOKENS, 2).astype(jnp.int32)


def place_ends(array, stream_key, least, top_value):
    longest = array.shape.index(max(array.shape))
    spots = []
    for shift in (0, 1):
        where = [jax.random.randint(jax.random.fold_in(stream_key, axis), (), 0, length) for axis, length in enumerate(array.shape)]
        where[longest] = (where[longest] + shift) % array.shape[longest]
        spots.append(tuple(where))
    return array.at[spots[0]].set(least).at[spots[1]].set(top_value)


def block_levels(rng, shape, pieces, smallest, high):
    gain, own = 1.0, jax.random.fold_in(rng, 6)
    for dim, parts in pieces:
        draws = jnp.exp(jax.random.uniform(jax.random.fold_in(own, dim), (parts,), jnp.float32, smallest / len(pieces), high / len(pieces)))
        gain = gain * jnp.repeat(draws, shape[dim] // parts).reshape([-1 if axis == dim else 1 for axis in range(len(shape))])
    return gain


def scatter_about(rng, shape, deviation, reach, cuts=(), held_as=jnp.bfloat16):
    level = block_levels(rng, shape, cuts, -0.22, 0.18) if cuts else 1.0
    array = jax.random.normal(rng, shape, jnp.float32) * deviation * level
    return jnp.minimum(jnp.maximum(array, -reach), reach).astype(held_as)


def setup_inputs(seed: int = 0) -> dict:
    arg_keys = jax.random.split(jax.random.key(seed), 8)
    tokens = scatter_about(arg_keys[0], (TOKENS, D), 1.0, 6.0, ((0, 16),))
    expert_ids = draw_expert_ids(jax.random.fold_in(arg_keys[7], 71), 0)
    gate_fixed = place_ends(jax.random.randint(arg_keys[2], (TOKENS, 2), 1, 32768), jax.random.fold_in(arg_keys[2], 1), 1, 32767).astype(jnp.int32)
    w_gate = scatter_about(arg_keys[3], (EXPERTS, D, FF), D ** -0.5, 0.09375, ((1, 16), (2, 16)))
    w_up = scatter_about(arg_keys[4], (EXPERTS, D, FF), D ** -0.5, 0.09375, ((1, 16), (2, 16)))
    w_down = scatter_about(arg_keys[5], (EXPERTS, FF, D), FF ** -0.5, 0.046875, ((1, 16), (2, 16)))
    d_out = scatter_about(arg_keys[6], (TOKENS, D), 1.0, 6.0, ((0, 16),))
    return {"tokens": tokens, "expert_ids": expert_ids, "gate_fixed": gate_fixed, "w_gate": w_gate, "w_up": w_up, "w_down": w_down, "d_out": d_out}


def route_table(expert_ids, gate_fixed, experts, capacity):
    expert_range = jnp.arange(experts, dtype=jnp.int32)
    picked = (expert_ids[None, :, :] == expert_range[:, None, None]).astype(jnp.int32)
    member = jnp.sum(picked, axis=2)
    scaled = jnp.sum(picked * gate_fixed[None, :, :], axis=2).astype(jnp.float32) / 32768.0
    before = jnp.cumsum(member, axis=1) - member
    slot_range = jnp.arange(capacity, dtype=jnp.int32)
    hit = (member[:, None, :] == 1) & (before[:, None, :] == slot_range[None, :, None])
    dispatch = hit.astype(jnp.float32)
    row_weight = jnp.sum(dispatch * scaled[:, None, :], axis=2)
    return dispatch, row_weight


def block_product(left, right):
    return jnp.dot(left, right, preferred_element_type=jnp.float32)


def reference(tokens, expert_ids, gate_fixed, w_gate, w_up, w_down, d_out):
    highest = lax.Precision.HIGHEST
    dispatch, row_weight = jax.vmap(lambda id_group, fixed_group: route_table(id_group, fixed_group, EXPERTS, CAP))(
        expert_ids.reshape(N_DP, TOK_DEV, 2), gate_fixed.reshape(N_DP, TOK_DEV, 2))
    token_groups = tokens.reshape(N_DP, TOK_DEV, D).astype(jnp.float32)
    grad_groups = d_out.reshape(N_DP, TOK_DEV, D).astype(jnp.float32)
    routed = jnp.einsum("gkct,gtd->gkcd", dispatch, token_groups, precision=highest).astype(jnp.bfloat16)
    d_rows = (row_weight[..., None] * jnp.einsum("gkct,gtd->gkcd", dispatch, grad_groups, precision=highest)).astype(jnp.bfloat16)
    down_list, back_list, grad_gate, grad_up, grad_down = [], [], [], [], []
    for expert in range(EXPERTS):
        rows_k = routed[:, expert].reshape(N_DP * CAP, D)
        grads_k = d_rows[:, expert].reshape(N_DP * CAP, D)
        gate = block_product(rows_k, w_gate[expert])
        up = block_product(rows_k, w_up[expert])
        sigma = jax.nn.sigmoid(gate)
        hidden = (gate * sigma * up).astype(jnp.bfloat16)
        down_list.append(jnp.dot(hidden, w_down[expert], preferred_element_type=jnp.float32))
        d_hidden = block_product(grads_k, w_down[expert].T)
        d_gate = (d_hidden * up * sigma * (1.0 + gate * (1.0 - sigma))).astype(jnp.bfloat16)
        d_up = (d_hidden * gate * sigma).astype(jnp.bfloat16)
        grad_down.append(jnp.dot(hidden.T, grads_k, preferred_element_type=jnp.float32))
        grad_gate.append(jnp.dot(rows_k.T, d_gate, preferred_element_type=jnp.float32))
        grad_up.append(jnp.dot(rows_k.T, d_up, preferred_element_type=jnp.float32))
        back = jnp.dot(d_gate, w_gate[expert].T, preferred_element_type=jnp.float32)
        back = back + jnp.dot(d_up, w_up[expert].T, preferred_element_type=jnp.float32)
        back_list.append(back)
    down_rows = jnp.stack(down_list, axis=0).reshape(EXPERTS, N_DP, CAP, D).transpose(1, 0, 2, 3)
    d_routed = jnp.stack(back_list, axis=0).reshape(EXPERTS, N_DP, CAP, D).transpose(1, 0, 2, 3)
    weighted = dispatch * row_weight[..., None]
    mixed = jnp.einsum("gkct,gkcd->gtd", weighted, down_rows, precision=highest).reshape(TOKENS, D)
    grad_tokens = jnp.einsum("gkct,gkcd->gtd", dispatch, d_routed, precision=highest).reshape(TOKENS, D)
    return (mixed, grad_tokens, jnp.stack(grad_gate, axis=0), jnp.stack(grad_up, axis=0), jnp.stack(grad_down, axis=0))
```

```python
import jax
import jax.numpy as jnp
import numpy as np
from jax import lax
from jax.sharding import Mesh, PartitionSpec as P

CAP = 32
DP = ("zl", "y")
ET = ("zh", "x", "c")
ALL = DP + ET
SIZES = (4, 4, 2, 4, 2)
F32 = jnp.float32
BF16 = jnp.bfloat16


def route_table(expert_ids, gate_fixed, experts, capacity):
    expert_range = jnp.arange(experts, dtype=jnp.int32)
    picked = (expert_ids[None, :, :] == expert_range[:, None, None]).astype(jnp.int32)
    member = jnp.sum(picked, axis=2)
    scaled = jnp.sum(picked * gate_fixed[None, :, :], axis=2).astype(F32) / 32768.0
    before = jnp.cumsum(member, axis=1) - member
    slot_range = jnp.arange(capacity, dtype=jnp.int32)
    hit = (member[:, None, :] == 1) & (before[:, None, :] == slot_range[None, :, None])
    dispatch = hit.astype(F32)
    row_weight = jnp.sum(dispatch * scaled[:, None, :], axis=2)
    return dispatch, row_weight


def exchange(values, axes):
    return lax.all_to_all(values, axes, split_axis=0, concat_axis=0, tiled=True)


def dot(spec, left, right):
    return jnp.einsum(spec, left, right, preferred_element_type=F32)


def local(tokens, expert_ids, gate_fixed, w_gate, w_up, w_down, d_out):
    highest = lax.Precision.HIGHEST
    experts, width, units = w_gate.shape
    n_zl, n_y = lax.axis_size("zl"), lax.axis_size("y")
    n_dp = n_zl * n_y
    n_q = lax.axis_size("x") * lax.axis_size("c")
    n_et = n_q * lax.axis_size("zh")
    rows = experts * CAP
    share = rows // n_q
    quarter = n_q // experts
    sub = units // n_y
    token_rows = tokens.shape[0]

    dispatch, row_weight = route_table(expert_ids, gate_fixed, experts, CAP)
    flat_dispatch = dispatch.reshape(rows, token_rows)
    flat_weight = row_weight.reshape(rows)

    place = lax.axis_index(("x", "c"))
    my_dispatch = lax.dynamic_slice_in_dim(flat_dispatch, place * share, share, 0).astype(BF16)
    my_weight = lax.dynamic_slice_in_dim(flat_weight, place * share, share, 0)
    my_routed = jnp.dot(my_dispatch, tokens, preferred_element_type=F32).astype(BF16)
    my_grads = (my_weight[:, None] * jnp.dot(my_dispatch, d_out, preferred_element_type=F32)).astype(BF16)
    both = jnp.stack([my_routed, my_grads])
    both = both.reshape(2, share, n_zl, n_y * width).transpose(2, 0, 1, 3)
    both = jnp.broadcast_to(both[:, None], (n_zl, n_y, 2, share, n_y * width))
    both = exchange(both.reshape(n_dp, 2, share, n_y * width), DP)
    both = lax.all_gather(both, ("x", "c"), axis=0)
    both = both.reshape(experts, quarter, n_dp, 2, share, n_y * width)
    routed = both[:, :, :, 0].reshape(experts, quarter * n_dp * share, n_y, width)
    grads = both[:, :, :, 1].reshape(experts, quarter * n_dp * share, n_y, width)

    turned = jnp.stack([w_gate.transpose(0, 2, 1), w_up.transpose(0, 2, 1), w_down])
    turned = turned.reshape(3, experts, n_y, sub, width).transpose(2, 0, 1, 3, 4)
    turned = exchange(turned, "y")
    first = dot("smkfd,krsd->kmfr", turned[:, :2], routed)
    second = dot("skfd,krsd->kfr", turned[:, 2], grads)
    part = jnp.concatenate([first, second[:, None]], axis=1)
    part = part.reshape(experts, 3, sub, quarter, n_dp * share).transpose(3, 0, 1, 2, 4)
    summed = jnp.sum(exchange(part.astype(BF16), "zl").astype(F32), axis=0)
    gate, up, d_hidden = summed[:, 0], summed[:, 1], summed[:, 2]
    sigma = jax.nn.sigmoid(gate)
    hidden = (gate * sigma * up).astype(BF16)
    d_gate = (d_hidden * up * sigma * (1.0 + gate * (1.0 - sigma))).astype(BF16)
    d_up = (d_hidden * gate * sigma).astype(BF16)
    acts = jnp.stack([hidden, d_gate, d_up])
    acts = lax.all_gather(acts, DP, axis=0).reshape(n_zl, n_y, 3, experts, sub, n_dp * share)
    hidden, d_gate, d_up = acts[:, :, 0], acts[:, :, 1], acts[:, :, 2]

    y = lax.axis_index("y")
    routed = lax.dynamic_index_in_dim(routed, y, 2, keepdims=False)
    grads = lax.dynamic_index_in_dim(grads, y, 2, keepdims=False)
    routed = routed.reshape(experts, quarter, n_dp * share, width)
    grads = grads.reshape(experts, quarter, n_dp * share, width)
    blocks_down = w_down.reshape(experts, n_y, sub, width)
    blocks_gate = w_gate.reshape(experts, width, n_y, sub)
    blocks_up = w_up.reshape(experts, width, n_y, sub)
    down = dot("zykfr,kyfd->kzrd", hidden, blocks_down)
    back = dot("zykfr,kdyf->kzrd", d_gate, blocks_gate)
    back = back + dot("zykfr,kdyf->kzrd", d_up, blocks_up)
    grad_down = dot("zykfr,kzrd->kyfd", hidden, grads).reshape(experts, units, width)
    grad_gate = dot("kzrd,zykfr->kdyf", routed, d_gate).reshape(experts, width, units)
    grad_up = dot("kzrd,zykfr->kdyf", routed, d_up).reshape(experts, width, units)

    sums = jnp.stack([down, back]).reshape(2, experts, quarter, n_dp, share, width)
    sums = sums.transpose(3, 0, 1, 2, 4, 5).reshape(n_dp, 2, rows, width)
    sums = jnp.sum(exchange(sums, ET), axis=0)
    home = [(i * n_et + j, j * n_dp + i) for i in range(n_dp) for j in range(n_et)]
    sums = lax.ppermute(sums, ALL, home)
    weighted = flat_dispatch * flat_weight[:, None]
    mixed = jnp.einsum("rt,rd->td", weighted, sums[0], precision=highest)
    grad_tokens = jnp.einsum("rt,rd->td", flat_dispatch, sums[1], precision=highest)
    return mixed, grad_tokens, grad_gate, grad_up, grad_down


def solution(mesh):
    fine = Mesh(np.asarray(mesh.devices).reshape(SIZES), ALL)
    placed = (
        P(DP, None),
        P(DP, None),
        P(DP, None),
        P(None, DP, ET),
        P(None, DP, ET),
        P(None, ET, DP),
        P(DP, None),
    )
    return jax.shard_map(
        local,
        mesh=fine,
        in_specs=placed,
        out_specs=(P(DP, ET), P(DP, ET), P(None, DP, ET), P(None, DP, ET), P(None, ET, DP)),
        check_vma=False,
    )
```

```python
import jax
import jax.numpy as jnp
import numpy as np
from jax import lax
from jax.experimental import pallas as pl
from jax.experimental.pallas import tpu as pltpu
from jax.sharding import Mesh, PartitionSpec as P

CAP = 32
DP = ("zl", "y")
ET = ("zh", "x", "c")
ALL = DP + ET
SIZES = (4, 4, 2, 4, 2)
F32 = jnp.float32
BF16 = jnp.bfloat16
VMEM = pltpu.CompilerParams(vmem_limit_bytes=48 * 2**20)
NT = (((1,), (1,)), ((), ()))
TN = (((0,), (0,)), ((), ()))


def route_table(expert_ids, gate_fixed, experts, capacity):
    expert_range = jnp.arange(experts, dtype=jnp.int32)
    picked = (expert_ids[None, :, :] == expert_range[:, None, None]).astype(jnp.int32)
    member = jnp.sum(picked, axis=2)
    scaled = jnp.sum(picked * gate_fixed[None, :, :], axis=2).astype(F32) / 32768.0
    before = jnp.cumsum(member, axis=1) - member
    slot_range = jnp.arange(capacity, dtype=jnp.int32)
    hit = (member[:, None, :] == 1) & (before[:, None, :] == slot_range[None, :, None])
    dispatch = hit.astype(F32)
    row_weight = jnp.sum(dispatch * scaled[:, None, :], axis=2)
    return dispatch, row_weight


def exchange(values, axes):
    return lax.all_to_all(values, axes, split_axis=0, concat_axis=0, tiled=True)


def shift(values, axis, step):
    return lax.ppermute(values, axis, [(i, (i + step) % 4) for i in range(4)])


def spread(values, axis):
    return [values] + [shift(values, axis, step) for step in (1, 2, 3)]


def spread_ring(values, axis):
    half = values.shape[0] // 2
    left, right = shift(values, axis, 1), shift(values, axis, 3)
    far = (shift(left[:half], axis, 1), shift(right[half:], axis, 3))
    return (values, left, right) + far


def dot(left, right, dims):
    return lax.dot_general(left, right, dims, preferred_element_type=F32)


def call(body, out_shape, inputs, scratch=(), flops=0):
    outs = jax.tree.leaves(out_shape)
    size = sum(int(np.prod(a.shape)) * a.dtype.itemsize for a in list(inputs) + outs)
    return pl.pallas_call(
        body,
        in_specs=[pl.BlockSpec(memory_space=pltpu.SMEM)]
        + [pl.BlockSpec(memory_space=pltpu.VMEM)] * (len(inputs) - 1),
        out_specs=jax.tree.map(lambda _: pl.BlockSpec(memory_space=pltpu.VMEM), out_shape),
        out_shape=out_shape,
        scratch_shapes=list(scratch),
        compiler_params=VMEM,
        cost_estimate=pl.CostEstimate(flops=flops, bytes_accessed=size, transcendentals=0),
    )(*inputs)


def pick_kernel(q_ref, dispatch_ref, weight_ref, tokens_ref, cotangent_ref, *out_refs):
    routed = jnp.dot(dispatch_ref[...], tokens_ref[...], preferred_element_type=F32)
    grads = jnp.dot(dispatch_ref[...], cotangent_ref[...], preferred_element_type=F32)
    routed = routed.astype(BF16)
    grads = (weight_ref[...] * grads).astype(BF16)
    for k in range(2):
        for y in range(4):
            out_refs[k][0, y, 0] = routed[k * CAP : (k + 1) * CAP]
            out_refs[k][0, y, 1] = grads[k * CAP : (k + 1) * CAP]


def pick_rows(q, dispatch, weight, tokens, cotangent):
    rows, count = dispatch.shape
    return pl.pallas_call(
        pick_kernel,
        grid_spec=pltpu.PrefetchScalarGridSpec(
            num_scalar_prefetch=1,
            grid=(4,),
            in_specs=[
                pl.BlockSpec((rows, count), lambda z, q: (0, 0)),
                pl.BlockSpec((rows, 1), lambda z, q: (0, 0)),
                pl.BlockSpec((count, 128), lambda z, q: (0, z * 8 + q[0])),
                pl.BlockSpec((count, 128), lambda z, q: (0, z * 8 + q[0])),
            ],
            out_specs=[pl.BlockSpec((1, 4, 2, CAP, 128), lambda z, q: (z, 0, 0, 0, 0))] * 2,
        ),
        out_shape=[jax.ShapeDtypeStruct((4, 4, 2, CAP, 128), BF16)] * 2,
        compiler_params=VMEM,
    )(q, dispatch, weight, tokens, cotangent)


def slot_rows(x_ref, column, t):
    return x_ref[column, :, t].reshape(16 * CAP, 128)


def first_kernel(where_ref, x_ref, w_ref, part_ref, own_ref):
    zl = where_ref[0]
    sub = w_ref.shape[2]
    sums = [None, None]
    for s in range(4):
        for t in range(2):
            rows = jnp.concatenate([slot_rows(x_ref, 2 * s + h, t) for h in range(2)], axis=1)
            if t == 0:
                units = jnp.concatenate([w_ref[s, 0], w_ref[s, 1]], axis=0)
            else:
                units = w_ref[s, 2]
            term = dot(units, rows, NT)
            sums[t] = term if sums[t] is None else sums[t] + term
    for which in range(3):
        value = sums[which // 2]
        value = value[sub : 2 * sub] if which == 1 else value[:sub]
        for z in range(4):
            block = value[:, z * 128 : (z + 1) * 128]
            part_ref[(z - zl + 4) % 4, which] = block.astype(BF16)

            @pl.when(zl == z)
            def _():
                own_ref[which] = block


def first_products(where, x, w):
    sub = w.shape[2]
    out_shape = [
        jax.ShapeDtypeStruct((4, 3, sub, 128), BF16),
        jax.ShapeDtypeStruct((3, sub, 128), F32),
    ]
    return call(first_kernel, out_shape, (where, x, w), flops=2 * 512 * 1024 * 3 * sub)


def lanes(where_ref, refs, far, step, which):
    zl = where_ref[0]
    ref = (refs[0], refs[1], far, refs[2])[step]
    return jnp.concatenate([ref[(zl - z + 4) % 4, which] for z in range(4)], axis=1)


def join_far(refs, far):
    half = refs[3].shape[0]
    far[:half] = refs[3][...]
    far[half:] = refs[4][...]


def sums_kernel(where_ref, w_ref, r0, r1, r2, r3, r4, sums_ref, far):
    y = where_ref[1]
    refs = (r0, r1, r2, r3, r4)
    join_far(refs, far)
    down, back = None, None
    for step in (0, 1, 3, 2):
        at = (y - step + 4) % 4
        term = dot(lanes(where_ref, refs, far, step, 0), w_ref[at, 2], TN)
        down = term if down is None else down + term
        term = dot(lanes(where_ref, refs, far, step, 1), w_ref[at, 0], TN)
        term = term + dot(lanes(where_ref, refs, far, step, 2), w_ref[at, 1], TN)
        back = term if back is None else back + term
    for g in range(16):
        sums_ref[g % 8, g // 8, 0] = down[g * CAP : (g + 1) * CAP]
        sums_ref[g % 8, g // 8, 1] = back[g * CAP : (g + 1) * CAP]


def unit_sums(where, w, pieces):
    sub, width = w.shape[2:]
    out_shape = jax.ShapeDtypeStruct((8, 2, 2, CAP, width), F32)
    scratch = [pltpu.VMEM(pieces[0].shape, BF16)]
    return call(
        sums_kernel, out_shape, (where, w, *pieces), scratch, flops=2 * 512 * 12 * sub * width
    )


def grads_kernel(where_ref, *refs):
    x_refs, piece_refs, out_refs = refs[:2], (refs[2:7], refs[7:12]), refs[12:15]
    fars, units = refs[15:17], refs[17]
    gate_ref, up_ref, down_ref = out_refs
    y = where_ref[1]
    sub = units.shape[2]
    for k in range(2):
        join_far(piece_refs[k], fars[k])
        rows = [
            jnp.concatenate([slot_rows(x_refs[k], h, t) for h in range(2)], axis=1)
            for t in range(2)
        ]
        turned = rows[0].T
        for which, out_ref in ((0, down_ref), (1, gate_ref), (2, up_ref)):
            for step in range(4):
                at = (y - step + 4) % 4
                units[2 * which + k, at] = lanes(where_ref, piece_refs[k], fars[k], step, which)
            block = units[2 * which + k].reshape(4 * sub, 16 * CAP)
            if which == 0:
                out_ref[k] = jnp.dot(block, rows[1], preferred_element_type=F32)
            else:
                out_ref[k] = dot(turned, block, NT)


def weight_grads(where, columns, pieces):
    sub = pieces[0][0].shape[2]
    out_shape = [
        jax.ShapeDtypeStruct((2, 256, 4 * sub), F32),
        jax.ShapeDtypeStruct((2, 256, 4 * sub), F32),
        jax.ShapeDtypeStruct((2, 4 * sub, 256), F32),
    ]
    scratch = [pltpu.VMEM(pieces[0][0].shape, BF16)] * 2
    scratch.append(pltpu.VMEM((6, 4, sub, 16 * CAP), BF16))
    inputs = (where, *columns, *pieces[0], *pieces[1])
    return call(grads_kernel, out_shape, inputs, scratch, flops=2 * 1024 * 12 * sub * 256)


def local(tokens, expert_ids, gate_fixed, w_gate, w_up, w_down, d_out):
    highest = lax.Precision.HIGHEST
    experts, width, units = w_gate.shape
    n_y, n_dp, n_et = 4, 16, 16
    rows = experts * CAP
    sub = units // n_y
    zl, y, zh = lax.axis_index("zl"), lax.axis_index("y"), lax.axis_index("zh")
    where = jnp.stack([zl, y]).astype(jnp.int32)

    dispatch, row_weight = route_table(expert_ids, gate_fixed, experts, CAP)
    flat_dispatch = dispatch.reshape(rows, tokens.shape[0])
    flat_weight = row_weight.reshape(rows)

    q = lax.axis_index(("x", "c")).astype(jnp.int32).reshape(1)
    picked = pick_rows(q, flat_dispatch.astype(BF16), flat_weight[:, None], tokens, d_out)
    pairs = [(i, j) for i in range(n_dp) for j in range(n_et)]
    home_same = [(i * n_et + j, j * n_dp + i) for i, j in pairs]
    home_other = [(i * n_et + j, (j ^ 8) * n_dp + i) for i, j in pairs]

    columns, pieces, sums = [], [], []
    for k in range(experts):
        both = exchange(picked[k].reshape(n_dp, 2, CAP, 128), DP)
        both = lax.all_gather(both, ("x", "c"), axis=0)
        columns.append(lax.dynamic_slice_in_dim(both, 2 * y, 2, 0))

        held = jnp.stack([w_gate[k].T, w_up[k].T, w_down[k]])
        held = held.reshape(3, n_y, sub, width).transpose(1, 0, 2, 3)
        turned = exchange(held, "y")
        part, summed = first_products(where, both, turned)
        for step in (1, 2, 3):
            summed = summed + shift(part[step], "zl", step).astype(F32)
        gate, up, d_hidden = summed[0], summed[1], summed[2]
        sigma = jax.nn.sigmoid(gate)
        hidden = (gate * sigma * up).astype(BF16)
        d_gate = (d_hidden * up * sigma * (1.0 + gate * (1.0 - sigma))).astype(BF16)
        d_up = (d_hidden * gate * sigma).astype(BF16)
        acts = jnp.stack([hidden, d_gate, d_up])
        pieces.append(spread_ring(jnp.stack(spread(acts, "zl")), "y"))
        part = unit_sums(where, held, pieces[k])

        part = jnp.sum(exchange(part, ("x", "c")), axis=0)
        same = lax.dynamic_index_in_dim(part, zh, 0, keepdims=False)
        other = lax.dynamic_index_in_dim(part, 1 - zh, 0, keepdims=False)
        sums.append(lax.ppermute(same, ALL, home_same) + lax.ppermute(other, ALL, home_other))

    grad_gate, grad_up, grad_down = weight_grads(where, columns, pieces)
    sums = jnp.concatenate(sums, axis=1)
    weighted = flat_dispatch * flat_weight[:, None]
    mixed = jnp.einsum("rt,rd->td", weighted, sums[0], precision=highest)
    grad_tokens = jnp.einsum("rt,rd->td", flat_dispatch, sums[1], precision=highest)
    return mixed, grad_tokens, grad_gate, grad_up, grad_down


def solution(mesh):
    fine = Mesh(np.asarray(mesh.devices).reshape(SIZES), ALL)
    placed = (
        P(DP, None),
        P(DP, None),
        P(DP, None),
        P(None, DP, ET),
        P(None, DP, ET),
        P(None, ET, DP),
        P(DP, None),
    )
    return jax.shard_map(
        local,
        mesh=fine,
        in_specs=placed,
        out_specs=(P(DP, ET), P(DP, ET), P(None, DP, ET), P(None, DP, ET), P(None, ET, DP)),
        check_vma=False,
    )
```

```python
import jax
import jax.numpy as jnp
import numpy as np
from jax import lax
from jax.experimental import pallas as pl
from jax.experimental.pallas import tpu as pltpu
from jax.sharding import Mesh, PartitionSpec as P

CAP = 32
DP = ("zl", "y")
ET = ("zh", "x", "c")
ALL = DP + ET
SIZES = (4, 4, 2, 4, 2)
F32 = jnp.float32
BF16 = jnp.bfloat16
VMEM = pltpu.CompilerParams(vmem_limit_bytes=48 * 2**20)
NT = (((1,), (1,)), ((), ()))
TN = (((0,), (0,)), ((), ()))


def route_table(expert_ids, gate_fixed, experts, capacity):
    expert_range = jnp.arange(experts, dtype=jnp.int32)
    picked = (expert_ids[None, :, :] == expert_range[:, None, None]).astype(jnp.int32)
    member = jnp.sum(picked, axis=2)
    scaled = jnp.sum(picked * gate_fixed[None, :, :], axis=2).astype(F32) / 32768.0
    before = jnp.cumsum(member, axis=1) - member
    slot_range = jnp.arange(capacity, dtype=jnp.int32)
    hit = (member[:, None, :] == 1) & (before[:, None, :] == slot_range[None, :, None])
    dispatch = hit.astype(F32)
    row_weight = jnp.sum(dispatch * scaled[:, None, :], axis=2)
    return dispatch, row_weight


def exchange(values, axes):
    return lax.all_to_all(values, axes, split_axis=0, concat_axis=0, tiled=True)


def shift(values, axis, step):
    return lax.ppermute(values, axis, [(i, (i + step) % 4) for i in range(4)])


def spread(values, axis):
    return [values] + [shift(values, axis, step) for step in (1, 2, 3)]


def after(values, *others):
    return lax.optimization_barrier((values, *others))[0]


def swap(values):
    return lax.ppermute(values, "c", [(0, 1), (1, 0)])


def dot(left, right, dims):
    return lax.dot_general(left, right, dims, preferred_element_type=F32)


def call(body, out_shape, inputs, scratch=(), flops=0):
    outs = jax.tree.leaves(out_shape)
    size = sum(int(np.prod(a.shape)) * a.dtype.itemsize for a in list(inputs) + outs)
    return pl.pallas_call(
        body,
        in_specs=[pl.BlockSpec(memory_space=pltpu.SMEM)]
        + [pl.BlockSpec(memory_space=pltpu.VMEM)] * (len(inputs) - 1),
        out_specs=jax.tree.map(lambda _: pl.BlockSpec(memory_space=pltpu.VMEM), out_shape),
        out_shape=out_shape,
        scratch_shapes=list(scratch),
        compiler_params=VMEM,
        cost_estimate=pl.CostEstimate(flops=flops, bytes_accessed=size, transcendentals=0),
    )(*inputs)


def pick_kernel(q_ref, dispatch_ref, weight_ref, tokens_ref, cotangent_ref, out_ref):
    routed = jnp.dot(dispatch_ref[...], tokens_ref[...], preferred_element_type=F32)
    grads = jnp.dot(dispatch_ref[...], cotangent_ref[...], preferred_element_type=F32)
    routed = routed.astype(BF16)
    grads = (weight_ref[...] * grads).astype(BF16)
    for y in range(4):
        out_ref[0, y, 0] = routed
        out_ref[0, y, 1] = grads


def pick_rows(q, dispatch, weight, tokens, cotangent):
    rows, count = dispatch.shape
    return pl.pallas_call(
        pick_kernel,
        grid_spec=pltpu.PrefetchScalarGridSpec(
            num_scalar_prefetch=1,
            grid=(4,),
            in_specs=[
                pl.BlockSpec((rows, count), lambda z, q: (0, 0)),
                pl.BlockSpec((rows, 1), lambda z, q: (0, 0)),
                pl.BlockSpec((count, 128), lambda z, q: (0, z * 8 + q[0])),
                pl.BlockSpec((count, 128), lambda z, q: (0, z * 8 + q[0])),
            ],
            out_specs=pl.BlockSpec((1, 4, 2, rows, 128), lambda z, q: (z, 0, 0, 0, 0)),
        ),
        out_shape=jax.ShapeDtypeStruct((4, 4, 2, rows, 128), BF16),
        compiler_params=VMEM,
    )(q, dispatch, weight, tokens, cotangent)


def turn_kernel(where_ref, gate_ref, up_ref, down_ref, *held_refs):
    for k, held_ref in enumerate(held_refs):
        sub = held_ref.shape[2]
        for which, ref in ((0, gate_ref), (1, up_ref)):
            held_ref[:, which] = ref[k].T.reshape(4, sub, ref.shape[1])
        held_ref[:, 2] = down_ref[k].reshape(4, sub, down_ref.shape[2])


def turn_weights(where, w_gate, w_up, w_down):
    experts, width, units = w_gate.shape
    out_shape = [jax.ShapeDtypeStruct((4, 3, units // 4, width), BF16)] * experts
    return call(turn_kernel, out_shape, (where, w_gate, w_up, w_down))


def slot_rows(x_ref, t):
    return jnp.concatenate([x_ref[h, :, t].reshape(16 * CAP, 128) for h in range(2)], axis=1)


def first_kernel(where_ref, x_ref, w_ref, part_ref, own_ref, total):
    zl, s = where_ref[0], pl.program_id(0)
    sub = w_ref.shape[2]
    routed, grads = [slot_rows(x_ref, t) for t in range(2)]
    first = dot(jnp.concatenate([w_ref[0, 0], w_ref[0, 1]], axis=0), routed, NT)
    second = dot(w_ref[0, 2], grads, NT)

    @pl.when(s == 0)
    def _():
        total[: 2 * sub] = first
        total[2 * sub :] = second

    @pl.when(s > 0)
    def _():
        total[: 2 * sub] += first
        total[2 * sub :] += second

    @pl.when(s == 3)
    def _():
        for which in range(3):
            for z in range(4):
                block = total[which * sub : (which + 1) * sub, z * 128 : (z + 1) * 128]
                part_ref[(z - zl + 4) % 4, which] = block.astype(BF16)

                @pl.when(zl == z)
                def _():
                    own_ref[which] = block


def first_products(where, x, w):
    sub, width = w.shape[2:]
    size = 2 * x.size + 2 * w.size + 10 * 3 * sub * 512
    return pl.pallas_call(
        first_kernel,
        grid_spec=pltpu.PrefetchScalarGridSpec(
            num_scalar_prefetch=1,
            grid=(4,),
            in_specs=[
                pl.BlockSpec((2, 16, 2, CAP, 128), lambda s, where: (s, 0, 0, 0, 0)),
                pl.BlockSpec((1, 3, sub, width), lambda s, where: (s, 0, 0, 0)),
            ],
            out_specs=[
                pl.BlockSpec((4, 3, sub, 128), lambda s, where: (0, 0, 0, 0)),
                pl.BlockSpec((3, sub, 128), lambda s, where: (0, 0, 0)),
            ],
            scratch_shapes=[pltpu.VMEM((3 * sub, 16 * CAP), F32)],
        ),
        out_shape=[
            jax.ShapeDtypeStruct((4, 3, sub, 128), BF16),
            jax.ShapeDtypeStruct((3, sub, 128), F32),
        ],
        compiler_params=VMEM,
        cost_estimate=pl.CostEstimate(
            flops=2 * 512 * 1024 * 3 * sub, bytes_accessed=size, transcendentals=0
        ),
    )(where, x, w)


def lanes(where_ref, refs, far, step, which):
    zl = where_ref[0]
    ref = (refs[0], refs[1], far, refs[2])[step]
    return jnp.concatenate([ref[(zl - z + 4) % 4, which] for z in range(4)], axis=1)


def join_far(refs, far):
    half = refs[3].shape[0]
    far[:half] = refs[3][...]
    far[half:] = refs[4][...]


def sums_kernel(where_ref, w_ref, r0, r1, r2, r3, r4, mine_ref, other_ref, far, held):
    y, x, c, zh = where_ref[1], where_ref[2], where_ref[3], where_ref[4]
    refs = (r0, r1, r2, r3, r4)
    join_far(refs, far)
    down, back = None, None
    for step in (0, 1, 3, 2):
        at = (y - step + 4) % 4
        term = dot(lanes(where_ref, refs, far, step, 0), w_ref[at, 2], TN)
        down = term if down is None else down + term
        term = dot(lanes(where_ref, refs, far, step, 1), w_ref[at, 0], TN)
        term = term + dot(lanes(where_ref, refs, far, step, 2), w_ref[at, 1], TN)
        back = term if back is None else back + term
    for g in range(16):
        held[g, 0] = down[g * CAP : (g + 1) * CAP]
        held[g, 1] = back[g * CAP : (g + 1) * CAP]
    for step in range(4):
        for turn in range(2):
            g = ((zh + turn) % 2) * 8 + ((x + step) % 4) * 2
            mine_ref[step, turn] = held[g + c]
            other_ref[step, turn] = held[g + 1 - c]


def unit_sums(where, w, pieces):
    sub, width = w.shape[2:]
    out_shape = [jax.ShapeDtypeStruct((4, 2, 2, CAP, width), F32)] * 2
    scratch = [pltpu.VMEM(pieces[0].shape, BF16), pltpu.VMEM((16, 2, CAP, width), F32)]
    return call(
        sums_kernel, out_shape, (where, w, *pieces), scratch, flops=2 * 512 * 12 * sub * width
    )


def grads_kernel(where_ref, *refs):
    x_refs, piece_refs, out_refs = refs[:2], (refs[2:7], refs[7:12]), refs[12:15]
    fars, units = refs[15:17], refs[17]
    gate_ref, up_ref, down_ref = out_refs
    y = where_ref[1]
    sub = units.shape[2]
    for k in range(2):
        join_far(piece_refs[k], fars[k])
        rows = [slot_rows(x_refs[k], t) for t in range(2)]
        turned = rows[0].T
        for which, out_ref in ((0, down_ref), (1, gate_ref), (2, up_ref)):
            for step in range(4):
                at = (y - step + 4) % 4
                units[2 * which + k, at] = lanes(where_ref, piece_refs[k], fars[k], step, which)
            block = units[2 * which + k].reshape(4 * sub, 16 * CAP)
            if which == 0:
                out_ref[k] = jnp.dot(block, rows[1], preferred_element_type=F32)
            else:
                out_ref[k] = dot(turned, block, NT)


def weight_grads(where, x, pieces):
    sub = pieces[0][0].shape[2]
    out_shape = [
        jax.ShapeDtypeStruct((2, 256, 4 * sub), F32),
        jax.ShapeDtypeStruct((2, 256, 4 * sub), F32),
        jax.ShapeDtypeStruct((2, 4 * sub, 256), F32),
    ]
    scratch = [pltpu.VMEM(pieces[0][0].shape, BF16)] * 2
    scratch.append(pltpu.VMEM((6, 4, sub, 16 * CAP), BF16))
    whole = pl.BlockSpec(memory_space=pltpu.VMEM)
    return pl.pallas_call(
        grads_kernel,
        grid_spec=pltpu.PrefetchScalarGridSpec(
            num_scalar_prefetch=1,
            grid=(1,),
            in_specs=[pl.BlockSpec((2, 16, 2, CAP, 128), lambda i, where: (where[1], 0, 0, 0, 0))] * 2
            + [whole] * 10,
            out_specs=[whole] * 3,
            scratch_shapes=scratch,
        ),
        out_shape=out_shape,
        compiler_params=VMEM,
        cost_estimate=pl.CostEstimate(
            flops=2 * 1024 * 12 * sub * 256, bytes_accessed=12 * 2**20, transcendentals=0
        ),
    )(where, *x, *pieces[0], *pieces[1])


def local(tokens, expert_ids, gate_fixed, w_gate, w_up, w_down, d_out):
    highest = lax.Precision.HIGHEST
    experts, width, units = w_gate.shape
    n_dp, n_et = 16, 16
    rows = experts * CAP
    where = jnp.stack([lax.axis_index(name) for name in ("zl", "y", "x", "c", "zh")]).astype(jnp.int32)

    dispatch, row_weight = route_table(expert_ids, gate_fixed, experts, CAP)
    flat_dispatch = dispatch.reshape(rows, tokens.shape[0])
    flat_weight = row_weight.reshape(rows)

    q = lax.axis_index(("x", "c")).astype(jnp.int32).reshape(1)
    picked = pick_rows(q, flat_dispatch.astype(BF16), flat_weight[:, None], tokens, d_out)
    pairs = [(i, j) for i in range(n_dp) for j in range(n_et)]
    home_same = [(i * n_et + j, j * n_dp + i) for i, j in pairs]
    home_other = [(i * n_et + j, (j ^ 8) * n_dp + i) for i, j in pairs]

    held = turn_weights(where, w_gate, w_up, w_down)
    turned = [exchange(each, "y") for each in held]
    sent = after(exchange(picked.reshape(n_dp, 2, rows, 128), DP), *held)
    x = [lax.all_gather(sent[:, :, k * CAP : (k + 1) * CAP], ("x", "c"), axis=0) for k in range(experts)]
    products = [first_products(where, x[k], turned[k]) for k in range(experts)]

    pieces, sums = [], []
    for k in range(experts):
        part, summed = products[k]
        for step in (1, 2, 3):
            summed = summed + shift(part[step], "zl", step).astype(F32)
        if k == 0:
            summed = after(summed, turned[1])
        gate, up, d_hidden = summed[0], summed[1], summed[2]
        sigma = jax.nn.sigmoid(gate)
        hidden = (gate * sigma * up).astype(BF16)
        d_gate = (d_hidden * up * sigma * (1.0 + gate * (1.0 - sigma))).astype(BF16)
        d_up = (d_hidden * gate * sigma).astype(BF16)
        acts = jnp.stack([hidden, d_gate, d_up])

        lines = jnp.stack(spread(acts, "zl"))
        if k == 0:
            lines = after(lines, products[1][0])
        left, right = shift(lines, "y", 1), shift(lines, "y", 3)
        half = lines.shape[0] // 2
        pieces.append([lines, left, right, shift(left[:half], "y", 1), shift(right[half:], "y", 3)])

    grads = weight_grads(where, x, pieces)
    for k in range(experts):
        if k:
            pieces[k][0] = after(pieces[k][0], part)
        own, other = unit_sums(where, held[k], pieces[k])
        own = own + swap(other)
        part = own[0]
        for step in (1, 2, 3):
            part = part + shift(own[step], "x", step)
        sums.append(part)
    sums = jnp.concatenate(sums, axis=2).astype(BF16)
    sums, *grads = lax.optimization_barrier((sums, *grads))
    same, other = lax.ppermute(sums[0], ALL, home_same), lax.ppermute(sums[1], ALL, home_other)
    sums = same.astype(F32) + other.astype(F32)

    grad_gate, grad_up, grad_down = grads
    weighted = flat_dispatch * flat_weight[:, None]
    mixed = jnp.einsum("rt,rd->td", weighted, sums[0], precision=highest)
    grad_tokens = jnp.einsum("rt,rd->td", flat_dispatch, sums[1], precision=highest)
    return mixed, grad_tokens, grad_gate, grad_up, grad_down


def solution(mesh):
    fine = Mesh(np.asarray(mesh.devices).reshape(SIZES), ALL)
    placed = (
        P(DP, None),
        P(DP, None),
        P(DP, None),
        P(None, DP, ET),
        P(None, DP, ET),
        P(None, ET, DP),
        P(DP, None),
    )
    return jax.shard_map(
        local,
        mesh=fine,
        in_specs=placed,
        out_specs=(P(DP, ET), P(DP, ET), P(None, DP, ET), P(None, DP, ET), P(None, ET, DP)),
        check_vma=False,
    )
```

```python
import jax
import jax.numpy as jnp
import numpy as np
from jax import lax
from jax.experimental import pallas as pl
from jax.experimental.pallas import tpu as pltpu
from jax.sharding import Mesh, PartitionSpec as P

CAP = 32
DP = ("zl", "y")
ET = ("zh", "x", "c")
ALL = DP + ET
SIZES = (4, 4, 2, 4, 2)
F32 = jnp.float32
BF16 = jnp.bfloat16
VMEM = pltpu.CompilerParams(vmem_limit_bytes=48 * 2**20)
NT = (((1,), (1,)), ((), ()))
TN = (((0,), (0,)), ((), ()))


def route_table(expert_ids, gate_fixed, experts, capacity):
    expert_range = jnp.arange(experts, dtype=jnp.int32)
    picked = (expert_ids[None, :, :] == expert_range[:, None, None]).astype(jnp.int32)
    member = jnp.sum(picked, axis=2)
    scaled = jnp.sum(picked * gate_fixed[None, :, :], axis=2).astype(F32) / 32768.0
    before = jnp.cumsum(member, axis=1) - member
    slot_range = jnp.arange(capacity, dtype=jnp.int32)
    hit = (member[:, None, :] == 1) & (before[:, None, :] == slot_range[None, :, None])
    dispatch = hit.astype(F32)
    row_weight = jnp.sum(dispatch * scaled[:, None, :], axis=2)
    return dispatch, row_weight


def exchange(values, axes):
    return lax.all_to_all(values, axes, split_axis=0, concat_axis=0, tiled=True)


def shift(values, axis, step):
    return lax.ppermute(values, axis, [(i, (i + step) % 4) for i in range(4)])


def spread(values, axis):
    return [values] + [shift(values, axis, step) for step in (1, 2, 3)]


def after(values, *others):
    return lax.optimization_barrier((values, *others))[0]


def swap(values):
    return lax.ppermute(values, "c", [(0, 1), (1, 0)])


def dot(left, right, dims):
    return lax.dot_general(left, right, dims, preferred_element_type=F32)


def call(body, out_shape, inputs, scratch=(), flops=0):
    outs = jax.tree.leaves(out_shape)
    size = sum(int(np.prod(a.shape)) * a.dtype.itemsize for a in list(inputs) + outs)
    return pl.pallas_call(
        body,
        in_specs=[pl.BlockSpec(memory_space=pltpu.SMEM)]
        + [pl.BlockSpec(memory_space=pltpu.VMEM)] * (len(inputs) - 1),
        out_specs=jax.tree.map(lambda _: pl.BlockSpec(memory_space=pltpu.VMEM), out_shape),
        out_shape=out_shape,
        scratch_shapes=list(scratch),
        compiler_params=VMEM,
        cost_estimate=pl.CostEstimate(flops=flops, bytes_accessed=size, transcendentals=0),
    )(*inputs)


def pick_kernel(q_ref, dispatch_ref, weight_ref, tokens_ref, cotangent_ref, out_ref, held, sems):
    q = q_ref[0]
    copies = []
    for z in range(4):
        for t, ref in enumerate((tokens_ref, cotangent_ref)):
            start = pl.multiple_of((z * 8 + q) * 128, 128)
            columns = ref.at[:, pl.ds(start, 128)]
            copies.append(pltpu.make_async_copy(columns, held.at[z, t], sems.at[z, t]))
            copies[-1].start()
    for z in range(4):
        copies[2 * z].wait()
        copies[2 * z + 1].wait()
        routed = jnp.dot(dispatch_ref[...], held[z, 0], preferred_element_type=F32)
        grads = jnp.dot(dispatch_ref[...], held[z, 1], preferred_element_type=F32)
        routed = routed.astype(BF16)
        grads = (weight_ref[...] * grads).astype(BF16)
        for y in range(4):
            out_ref[z, y, 0] = routed
            out_ref[z, y, 1] = grads


def pick_rows(q, dispatch, weight, tokens, cotangent):
    rows, count = dispatch.shape
    return pl.pallas_call(
        pick_kernel,
        in_specs=[pl.BlockSpec(memory_space=pltpu.SMEM)]
        + [pl.BlockSpec(memory_space=pltpu.VMEM)] * 2
        + [pl.BlockSpec(memory_space=pltpu.HBM)] * 2,
        out_specs=pl.BlockSpec(memory_space=pltpu.VMEM),
        out_shape=jax.ShapeDtypeStruct((4, 4, 2, rows, 128), BF16),
        scratch_shapes=[pltpu.VMEM((4, 2, count, 128), BF16), pltpu.SemaphoreType.DMA((4, 2))],
        compiler_params=pltpu.CompilerParams(vmem_limit_bytes=61 * 2**20),
    )(q, dispatch, weight, tokens, cotangent)


def turn_kernel(where_ref, gate_ref, up_ref, down_ref, *held_refs):
    for k, held_ref in enumerate(held_refs):
        sub = held_ref.shape[2]
        for which, ref in ((0, gate_ref), (1, up_ref)):
            held_ref[:, which] = ref[k].T.reshape(4, sub, ref.shape[1])
        held_ref[:, 2] = down_ref[k].reshape(4, sub, down_ref.shape[2])


def turn_weights(where, w_gate, w_up, w_down):
    experts, width, units = w_gate.shape
    out_shape = [jax.ShapeDtypeStruct((4, 3, units // 4, width), BF16)] * experts
    return call(turn_kernel, out_shape, (where, w_gate, w_up, w_down))


def slot_rows(x_ref, t):
    return jnp.concatenate([x_ref[h, :, t].reshape(16 * CAP, 128) for h in range(2)], axis=1)


def first_kernel(where_ref, x_ref, w_ref, part_ref, own_ref, total):
    zl, s = where_ref[0], pl.program_id(0)
    sub = w_ref.shape[2]
    routed, grads = [slot_rows(x_ref, t) for t in range(2)]
    first = dot(jnp.concatenate([w_ref[0, 0], w_ref[0, 1]], axis=0), routed, NT)
    second = dot(w_ref[0, 2], grads, NT)

    @pl.when(s == 0)
    def _():
        total[: 2 * sub] = first
        total[2 * sub :] = second

    @pl.when(s > 0)
    def _():
        total[: 2 * sub] += first
        total[2 * sub :] += second

    @pl.when(s == 3)
    def _():
        for which in range(3):
            for z in range(4):
                block = total[which * sub : (which + 1) * sub, z * 128 : (z + 1) * 128]
                part_ref[(z - zl + 4) % 4, which] = block.astype(BF16)

                @pl.when(zl == z)
                def _():
                    own_ref[which] = block


def first_products(where, x, w):
    sub, width = w.shape[2:]
    size = 2 * x.size + 2 * w.size + 10 * 3 * sub * 512
    return pl.pallas_call(
        first_kernel,
        grid_spec=pltpu.PrefetchScalarGridSpec(
            num_scalar_prefetch=1,
            grid=(4,),
            in_specs=[
                pl.BlockSpec((2, 16, 2, CAP, 128), lambda s, where: (s, 0, 0, 0, 0)),
                pl.BlockSpec((1, 3, sub, width), lambda s, where: (s, 0, 0, 0)),
            ],
            out_specs=[
                pl.BlockSpec((4, 3, sub, 128), lambda s, where: (0, 0, 0, 0)),
                pl.BlockSpec((3, sub, 128), lambda s, where: (0, 0, 0)),
            ],
            scratch_shapes=[pltpu.VMEM((3 * sub, 16 * CAP), F32)],
        ),
        out_shape=[
            jax.ShapeDtypeStruct((4, 3, sub, 128), BF16),
            jax.ShapeDtypeStruct((3, sub, 128), F32),
        ],
        compiler_params=VMEM,
        cost_estimate=pl.CostEstimate(
            flops=2 * 512 * 1024 * 3 * sub, bytes_accessed=size, transcendentals=0
        ),
    )(where, x, w)


def lanes(where_ref, refs, far, step, which):
    zl = where_ref[0]
    ref = (refs[0], refs[1], far, refs[2])[step]
    return jnp.concatenate([ref[(zl - z + 4) % 4, which] for z in range(4)], axis=1)


def join_far(refs, far):
    half = refs[3].shape[0]
    far[:half] = refs[3][...]
    far[half:] = refs[4][...]


def sums_kernel(where_ref, w_ref, r0, r1, r2, r3, r4, mine_ref, other_ref, far, held):
    y, x, c, zh = where_ref[1], where_ref[2], where_ref[3], where_ref[4]
    refs = (r0, r1, r2, r3, r4)
    join_far(refs, far)
    down, back = None, None
    for step in (0, 1, 3, 2):
        at = (y - step + 4) % 4
        term = dot(lanes(where_ref, refs, far, step, 0), w_ref[at, 2], TN)
        down = term if down is None else down + term
        term = dot(lanes(where_ref, refs, far, step, 1), w_ref[at, 0], TN)
        term = term + dot(lanes(where_ref, refs, far, step, 2), w_ref[at, 1], TN)
        back = term if back is None else back + term
    for g in range(16):
        held[g, 0] = down[g * CAP : (g + 1) * CAP]
        held[g, 1] = back[g * CAP : (g + 1) * CAP]
    for step in range(4):
        for turn in range(2):
            g = ((zh + turn) % 2) * 8 + ((x + step) % 4) * 2
            mine_ref[step, turn] = held[g + c]
            other_ref[step, turn] = held[g + 1 - c]


def unit_sums(where, w, pieces):
    sub, width = w.shape[2:]
    out_shape = [jax.ShapeDtypeStruct((4, 2, 2, CAP, width), F32)] * 2
    scratch = [pltpu.VMEM(pieces[0].shape, BF16), pltpu.VMEM((16, 2, CAP, width), F32)]
    return call(
        sums_kernel, out_shape, (where, w, *pieces), scratch, flops=2 * 512 * 12 * sub * width
    )


def grads_kernel(where_ref, *refs):
    x_refs, piece_refs, out_refs = refs[:2], (refs[2:7], refs[7:12]), refs[12:15]
    fars, units = refs[15:17], refs[17]
    gate_ref, up_ref, down_ref = out_refs
    y = where_ref[1]
    sub = units.shape[2]
    for k in range(2):
        join_far(piece_refs[k], fars[k])
        rows = [slot_rows(x_refs[k], t) for t in range(2)]
        turned = rows[0].T
        for which, out_ref in ((0, down_ref), (1, gate_ref), (2, up_ref)):
            for step in range(4):
                at = (y - step + 4) % 4
                units[2 * which + k, at] = lanes(where_ref, piece_refs[k], fars[k], step, which)
            block = units[2 * which + k].reshape(4 * sub, 16 * CAP)
            if which == 0:
                out_ref[k] = jnp.dot(block, rows[1], preferred_element_type=F32)
            else:
                out_ref[k] = dot(turned, block, NT)


def weight_grads(where, x, pieces):
    sub = pieces[0][0].shape[2]
    out_shape = [
        jax.ShapeDtypeStruct((2, 256, 4 * sub), F32),
        jax.ShapeDtypeStruct((2, 256, 4 * sub), F32),
        jax.ShapeDtypeStruct((2, 4 * sub, 256), F32),
    ]
    scratch = [pltpu.VMEM(pieces[0][0].shape, BF16)] * 2
    scratch.append(pltpu.VMEM((6, 4, sub, 16 * CAP), BF16))
    whole = pl.BlockSpec(memory_space=pltpu.VMEM)
    return pl.pallas_call(
        grads_kernel,
        grid_spec=pltpu.PrefetchScalarGridSpec(
            num_scalar_prefetch=1,
            grid=(1,),
            in_specs=[pl.BlockSpec((2, 16, 2, CAP, 128), lambda i, where: (where[1], 0, 0, 0, 0))] * 2
            + [whole] * 10,
            out_specs=[whole] * 3,
            scratch_shapes=scratch,
        ),
        out_shape=out_shape,
        compiler_params=VMEM,
        cost_estimate=pl.CostEstimate(
            flops=2 * 1024 * 12 * sub * 256, bytes_accessed=12 * 2**20, transcendentals=0
        ),
    )(where, *x, *pieces[0], *pieces[1])


def local(tokens, expert_ids, gate_fixed, w_gate, w_up, w_down, d_out):
    highest = lax.Precision.HIGHEST
    experts, width, units = w_gate.shape
    n_dp, n_et = 16, 16
    rows = experts * CAP
    where = jnp.stack([lax.axis_index(name) for name in ("zl", "y", "x", "c", "zh")]).astype(jnp.int32)

    dispatch, row_weight = route_table(expert_ids, gate_fixed, experts, CAP)
    flat_dispatch = dispatch.reshape(rows, tokens.shape[0])
    flat_weight = row_weight.reshape(rows)

    q = lax.axis_index(("x", "c")).astype(jnp.int32).reshape(1)
    picked = pick_rows(q, flat_dispatch.astype(BF16), flat_weight[:, None], tokens, d_out)
    pairs = [(i, j) for i in range(n_dp) for j in range(n_et)]
    home_same = [(i * n_et + j, j * n_dp + i) for i, j in pairs]
    home_other = [(i * n_et + j, (j ^ 8) * n_dp + i) for i, j in pairs]

    held = turn_weights(where, w_gate, w_up, w_down)
    turned = [exchange(each, "y") for each in held]
    sent = after(exchange(picked.reshape(n_dp, 2, rows, 128), DP), *held)
    x = [lax.all_gather(sent[:, :, k * CAP : (k + 1) * CAP], ("x", "c"), axis=0) for k in range(experts)]
    products = [first_products(where, x[k], turned[k]) for k in range(experts)]

    pieces, sums = [], []
    for k in range(experts):
        part, summed = products[k]
        for step in (1, 2, 3):
            summed = summed + shift(part[step], "zl", step).astype(F32)
        if k == 0:
            summed = after(summed, turned[1])
        gate, up, d_hidden = summed[0], summed[1], summed[2]
        sigma = jax.nn.sigmoid(gate)
        hidden = (gate * sigma * up).astype(BF16)
        d_gate = (d_hidden * up * sigma * (1.0 + gate * (1.0 - sigma))).astype(BF16)
        d_up = (d_hidden * gate * sigma).astype(BF16)
        acts = jnp.stack([hidden, d_gate, d_up])

        lines = jnp.stack(spread(acts, "zl"))
        if k == 0:
            lines = after(lines, products[1][0])
        left, right = shift(lines, "y", 1), shift(lines, "y", 3)
        half = lines.shape[0] // 2
        pieces.append([lines, left, right, shift(left[:half], "y", 1), shift(right[half:], "y", 3)])

    grads = weight_grads(where, x, pieces)
    for k in range(experts):
        if k:
            pieces[k][0] = after(pieces[k][0], part)
        own, other = unit_sums(where, held[k], pieces[k])
        own = own + swap(other)
        part = own[0]
        for step in (1, 2, 3):
            part = part + shift(own[step], "x", step)
        sums.append(part)
    sums = jnp.concatenate(sums, axis=2).astype(BF16)
    sums, *grads = lax.optimization_barrier((sums, *grads))
    same, other = lax.ppermute(sums[0], ALL, home_same), lax.ppermute(sums[1], ALL, home_other)
    sums = same.astype(F32) + other.astype(F32)

    grad_gate, grad_up, grad_down = grads
    weighted = flat_dispatch * flat_weight[:, None]
    mixed = jnp.einsum("rt,rd->td", weighted, sums[0], precision=highest)
    grad_tokens = jnp.einsum("rt,rd->td", flat_dispatch, sums[1], precision=highest)
    return mixed, grad_tokens, grad_gate, grad_up, grad_down


def solution(mesh):
    fine = Mesh(np.asarray(mesh.devices).reshape(SIZES), ALL)
    placed = (
        P(DP, None),
        P(DP, None),
        P(DP, None),
        P(None, DP, ET),
        P(None, DP, ET),
        P(None, ET, DP),
        P(DP, None),
    )
    return jax.shard_map(
        local,
        mesh=fine,
        in_specs=placed,
        out_specs=(P(DP, ET), P(DP, ET), P(None, DP, ET), P(None, DP, ET), P(None, ET, DP)),
        check_vma=False,
    )
```
